32 devices in a mesh: expert: 4 (over y, x), dp: 4 (over z), tensor: 2 (over core).
Axes of the slice: x: 2, y: 2, z: 4, core: 2. Of those that a mesh axis runs over, the one named last changes fastest.
Arguments:
- tokens: bfloat16 [16384, 768], P(('expert', 'dp')), may hold values from -6 to 6
- lengths: int32 [16, 4], P(('expert', 'dp')), may hold values from 1 to 768, 1024 in all within a row
- routes: int32 [16384, 1], P(('expert', 'dp')), may hold values from 0 to 7; in each aligned block of 1024 rows (0 to 1023, 1024 to 2047, ...) at most 256 rows name the same one
- cotangent: bfloat16 [16384, 768], P(('expert', 'dp')), may hold values from -6 to 6
- norm_gains: float32 [2, 768], replicated, may hold values from 0.5 to 1.5
- attn_biases: float32 [3, 768], replicated, may hold values from -1.75 to 1.75
- w_attn: float32 [3, 768, 768], P(None, None, 'tensor'), may hold values from -0.3125 to 0.3125
- w_proj: float32 [768, 768], P('tensor'), may hold values from -0.625 to 0.625
- w_router: float32 [768, 8], replicated, may hold values from -0.109375 to 0.109375
- w_in: float32 [8, 768, 3072], P('expert', 'dp', 'tensor'), may hold values from -0.21875 to 0.21875
- w_out: float32 [8, 768, 3072], P('expert', 'dp', 'tensor'), may hold values from -2.5 to 2.5
- gains_moment: float32 [2, 768], replicated, may hold values from -160 to 160
- biases_moment: float32 [3, 768], replicated, may hold values from -160 to 160
- attn_moment: float32 [3, 768, 768], P(None, None, 'tensor'), may hold values from -1024 to 1024
- proj_moment: float32 [768, 768], P('tensor'), may hold values from -320 to 320
- router_moment: float32 [768, 8], replicated, may hold values from -32768 to 32768
- in_moment: float32 [8, 768, 3072], P('expert', 'dp', 'tensor'), may hold values from -224 to 224
- out_moment: float32 [8, 768, 3072], P('expert', 'dp', 'tensor'), may hold values from -20 to 20
Outputs:
- layer_out: bfloat16 [16384, 768], P(('expert', 'dp'))
- input_grad: float32 [16384, 768], P(('expert', 'dp'))
- expert_branch: float32 [16384, 768], P(('expert', 'dp'))
- updated_norm_gains: float32 [2, 768], replicated
- new_gains_moment: float32 [2, 768], replicated
- new_biases: float32 [3, 768], replicated
- new_biases_moment: float32 [3, 768], replicated
- new_attn: float32 [3, 768, 768], P(None, None, 'tensor')
- new_attn_moment: float32 [3, 768, 768], P(None, None, 'tensor')
- new_proj: float32 [768, 768], P('tensor')
- new_proj_moment: float32 [768, 768], P('tensor')
- new_router: float32 [768, 8], replicated
- new_router_moment: float32 [768, 8], replicated
- new_in: float32 [8, 768, 3072], P('expert', 'dp', 'tensor')
- new_in_moment: float32 [8, 768, 3072], P('expert', 'dp', 'tensor')
- new_out: float32 [8, 768, 3072], P('expert', 'dp', 'tensor')
- new_out_moment: float32 [8, 768, 3072], P('expert', 'dp', 'tensor')
The draws below stay inside these ranges and needn't reach their ends.
Inputs may be any that keep to these rules, and one draw needn't show every extreme that they name: `routes`: within each data group (aligned blocks of 1024 rows) no expert is named by more than 256 tokens, and in some groups one expert is named by exactly 256. Row g holds the lengths of the 4 sequences of data group g in the order in which they lie; they sum to 1024 and the largest is 768.
All inputs are finite; a program needn't handle non-finite values.
Results may differ from the reference program's by a relative error of at most 0.025.
The reference program's roundings to bfloat16 on the way count: a program that leaves them out, or rounds other values in their place, can miss the bound.
Values may be sent and summed in bfloat16 or wider, within the bound.
A program may use at most 256 MiB of HBM per device.

```python
import math
import jax
import jax.numpy as jnp
import numpy as np
from jax import lax

D = 768
HEADS = 12
HD = 64
FF = 3072
ROWS = 1024
NSEQ = 4
NS_STEPS = 5
EXPERTS = 8
GROUPS = 16
TOKENS = 16384
CAP = 256
LONGEST = 768


def level_of(stream_key, extent, shards, low, high):
    gain = 1.0
    for dim, parts in shards:
        steps = jax.random.uniform(jax.random.fold_in(jax.random.fold_in(stream_key, 6), dim), (parts,), jnp.float32, low / len(shards), high / len(shards))
        gain = gain * jnp.repeat(jnp.exp(steps), extent[dim] // parts).reshape((-1,) + (1,) * (len(extent) - 1 - dim))
    return gain


def length_profile(number_of, total, limit, lean):
    portions = [(1 << 20) // math.isqrt(rank ** lean) + 1 for rank in range(2, number_of + 1)]
    rest, given = total - limit - (number_of - 1), [1] * (number_of - 1)
    while rest > 0:
        free = [i for i in range(number_of - 1) if given[i] < limit]
        mass, budget = sum([portions[i] for i in free]), rest
        for i in free:
            more = min(limit - given[i], max(1, budget * portions[i] // mass), rest)
            given[i] = given[i] + more
            rest = rest - more
    return np.array([limit] + given)


def ragged(own_key, count, total, bound, slope):
    if count == 2:
        one = jax.random.randint(own_key, (), max(1, total - bound), min(bound, total - 1) + 1)
        return jnp.stack([one, total - one])
    sizes = jnp.asarray(length_profile(count, total, bound, slope), jnp.int32)
    couples = (count - 1) // 2
    source_of, sink = sizes[1:1 + 2 * couples:2], sizes[2:2 + 2 * couples:2]
    slack = jnp.minimum(source_of - 1, bound - sink)
    moved = jax.random.randint(jax.random.fold_in(own_key, 1), (couples,), 0, 1 << 20) % (slack + 1)
    sizes = sizes.at[1:1 + 2 * couples:2].set(source_of - moved).at[2:2 + 2 * couples:2].set(sink + moved)
    return sizes[jax.random.permutation(jax.random.fold_in(own_key, 2), count)]


def routed_block(stream_key, own, number, rows, amount, top, bound, lean):
    order = jax.random.permutation(stream_key, amount)
    packed, common = load_shares(amount, rows * top, bound, lean, True), load_shares(amount, rows * top, bound, lean, False)
    places = jnp.arange(amount)

    def named(sizes, turn):
        used = int((sizes > 0).sum())
        fixed = max(1, used // 4)
        shifted = fixed + (places - fixed + turn * (used - fixed)) % max(1, amount - fixed)
        return jnp.zeros((amount,), jnp.int32).at[order[jnp.where(places < fixed, places, shifted)]].set(jnp.asarray(sizes, jnp.int32))

    sizes = jnp.where(number % 4 == 0, named(packed, number // 4), named(common, number - number // 4 - 1))
    mixed = jax.random.permutation(jax.random.fold_in(own, 3), amount)
    giver, receiver = mixed[0:amount // 2 * 2:2], mixed[1:amount // 2 * 2:2]
    room = jnp.minimum(sizes[giver] - 1, bound - sizes[receiver]) // 2
    room = jnp.where((giver == order[0]) | (receiver == order[0]) | (sizes[receiver] == 0), 0, jnp.maximum(room, 0))
    shifted = jax.random.randint(jax.random.fold_in(own, 4), (amount // 2,), 0, 1 << 20) % (room + 1)
    sizes = sizes.at[giver].add(-shifted).at[receiver].add(shifted)
    members = jnp.searchsorted(jnp.cumsum(sizes), jnp.arange(rows * top), side="right").astype(jnp.int32)
    table = members.reshape(top, rows).T
    table = table[jax.random.permutation(jax.random.fold_in(own, 1), rows)]
    turn = jax.random.randint(jax.random.fold_in(own, 2), (rows, 1), 0, top)
    return jnp.take_along_axis(table, (jnp.arange(top)[None, :] + turn) % top, axis=1)


def load_shares(amount, total, most, slope, full):
    loads = [(1 << 20) // math.isqrt(rank ** slope) + 1 for rank in range(1, amount + 1)]
    largest = most if full else min(most, max(-(-total // amount), total * loads[0] // sum(loads)))
    least = 1 if total - largest >= amount - 1 else 0
    counts, spare = [largest] + [least] * (amount - 1), total - largest - least * (amount - 1)
    while spare > 0:
        movable = [i for i in range(1, amount) if counts[i] < largest] or [i for i in range(1, amount) if counts[i] < most]
        pool, budget = sum([loads[i] for i in movable]), spare
        for i in movable:
            extra = min(most - counts[i], max(1, budget * loads[i] // pool), spare)
            counts[i] = counts[i] + extra
            spare = spare - extra
    return np.array(counts)


def scatter_about(stream_key, shape, spread, most, cuts=(), kind=jnp.bfloat16):
    values = spread * jax.random.normal(stream_key, shape, jnp.float32)
    if cuts:
        values = values * level_of(stream_key, shape, cuts, -0.22, 0.18)
    return jnp.clip(values, -most, most).astype(kind)


def setup_inputs(seed: int = 0) -> dict:
    arg_keys = jax.random.split(jax.random.key(seed), 19)
    tokens = scatter_about(arg_keys[0], (TOKENS, D), 1.0, 6.0, ((0, 16),))
    lengths = jax.vmap(lambda own: ragged(own, NSEQ, ROWS, LONGEST, 2))(jax.random.split(arg_keys[1], GROUPS)).reshape((GROUPS, NSEQ)).astype(jnp.int32)
    routes_keys = jax.random.split(jax.random.fold_in(arg_keys[2], 1), TOKENS // ROWS)
    routes_turns = jax.random.permutation(jax.random.fold_in(arg_keys[2], 3), TOKENS // ROWS)
    routes = jax.vmap(lambda own, number: routed_block(jax.random.fold_in(arg_keys[2], 2), own, number, ROWS, EXPERTS, 1, CAP, 2))(routes_keys, routes_turns).reshape((TOKENS, 1))
    cotangent = scatter_about(arg_keys[3], (TOKENS, D), 1.0, 6.0, ((0, 16),))
    norm_gains = jnp.clip(1.0 + 0.1 * jax.random.normal(arg_keys[4], (2, D), jnp.float32), 0.5, 1.5)
    attn_biases = scatter_about(arg_keys[5], (3, D), 0.3, 1.75, (), jnp.float32)
    w_attn = scatter_about(arg_keys[6], (3, D, D), 0.05, 0.3125, ((2, 2),), jnp.float32)
    w_proj = scatter_about(arg_keys[7], (D, D), 0.1, 0.625, ((0, 2),), jnp.float32)
    w_router = scatter_about(arg_keys[8], (D, EXPERTS), (0.5 * D ** -0.5), 0.109375, (), jnp.float32)
    w_in = scatter_about(arg_keys[9], (EXPERTS, D, FF), D ** -0.5, 0.21875, ((0, 4), (1, 4), (2, 2)), jnp.float32)
    w_out = scatter_about(arg_keys[10], (EXPERTS, D, FF), 0.4, 2.5, ((0, 4), (1, 4), (2, 2)), jnp.float32)
    gains_moment = scatter_about(arg_keys[11], (2, D), (0.2 * TOKENS ** 0.5), 160.0, (), jnp.float32)
    biases_moment = scatter_about(arg_keys[12], (3, D), (0.2 * TOKENS ** 0.5), 160.0, (), jnp.float32)
    attn_moment = scatter_about(arg_keys[13], (3, D, D), (1.5 * TOKENS ** 0.5), 1024.0, ((2, 2),), jnp.float32)
    proj_moment = scatter_about(arg_keys[14], (D, D), (0.4 * TOKENS ** 0.5), 320.0, ((0, 2),), jnp.float32)
    router_moment = scatter_about(arg_keys[15], (D, EXPERTS), (0.25 * (FF * D * TOKENS) ** 0.5 / EXPERTS), 32768.0, (), jnp.float32)
    in_moment = scatter_about(arg_keys[16], (EXPERTS, D, FF), (0.25 * D ** 0.5 / EXPERTS * (TOKENS / EXPERTS) ** 0.5), 224.0, ((0, 4), (1, 4), (2, 2)), jnp.float32)
    out_moment = scatter_about(arg_keys[17], (EXPERTS, D, FF), (0.6 / EXPERTS * (TOKENS / EXPERTS) ** 0.5), 20.0, ((0, 4), (1, 4), (2, 2)), jnp.float32)
    return dict(tokens=tokens, lengths=lengths, routes=routes, cotangent=cotangent, norm_gains=norm_gains, attn_biases=attn_biases, w_attn=w_attn, w_proj=w_proj, w_router=w_router, w_in=w_in, w_out=w_out, gains_moment=gains_moment, biases_moment=biases_moment, attn_moment=attn_moment, proj_moment=proj_moment, router_moment=router_moment, in_moment=in_moment, out_moment=out_moment)


PRECISE = lax.Precision.HIGHEST
MOMENT = 0.95
VECTOR_DECAY = 0.9
VECTOR_RATE = 0.2
COEF_A = 3.4445
COEF_B = -4.775
COEF_C = 2.0315
RATE_ATTN = 0.05
RATE_PROJ = 0.1
RATE_ROUTER = 0.03
RATE_IN = 0.04
RATE_OUT = 0.4

@jax.custom_vjp
def low(v):
    return lax.optimization_barrier(v.astype(jnp.bfloat16)).astype(jnp.float32)

@jax.custom_vjp
def low_back(v):
    return v

def low_keep(v):
    return (low(v), None)

def low_pass(kept, grad):
    return (grad,)

def back_keep(v):
    return (v, None)

def back_low(kept, grad):
    return (low(grad),)
low.defvjp(low_keep, low_pass)
low_back.defvjp(back_keep, back_low)

def both_ways(values):
    return low(low_back(values))

def rms_norm(values, gain_row):
    factor = lax.rsqrt(lax.optimization_barrier(jnp.mean(values * values, axis=-1, keepdims=True)) + 1e-06)
    return values * factor * gain_row

def sequence_ids(lengths, count):
    seq_ends = jnp.cumsum(lengths, axis=-1)
    position = jnp.arange(count, dtype=jnp.int32)
    return lax.optimization_barrier(jnp.sum((position[:, None][None] >= seq_ends[:, None, :]).astype(jnp.int32), axis=-1))

def slot_index(route_ids, count):
    onehot = (route_ids[..., None] == jnp.arange(count, dtype=jnp.int32)).astype(jnp.int32)
    return lax.optimization_barrier(jnp.sum((jnp.cumsum(onehot, axis=-2) - 1) * onehot, axis=-1))

def attention_forward(pieces):
    query, keyset, valueset, segment = pieces
    query_heads = query.reshape(ROWS, HEADS, HD)
    key_heads = keyset.reshape(ROWS, HEADS, HD)
    value_heads = valueset.reshape(ROWS, HEADS, HD)
    scores = jnp.einsum('qhd,khd->hqk', query_heads, key_heads, precision=PRECISE) * HD ** (-0.5)
    same_seq = segment[:, None] == segment[None, :]
    scores = low_back(jnp.where(same_seq[None], scores, -1e+30))
    weights = low(jax.nn.softmax(scores, axis=-1))
    heads_out = jnp.einsum('hqk,khd->qhd', weights, value_heads, precision=PRECISE)
    return both_ways(heads_out.reshape(ROWS, D))

def expert_block(pieces):
    inputs, weight_in, weight_out = pieces
    preact = low_back(jnp.dot(inputs, low(weight_in), precision=PRECISE))
    activation = low(jax.nn.gelu(preact))
    return both_ways(jnp.dot(activation, low(weight_out).T, precision=PRECISE))

def layer(tokens_f, norm_gains, attn_biases, w_attn, w_proj, w_router, w_in, w_out, segment, route_ids, slot_ids):
    groups = tokens_f.shape[0]
    normed = low(rms_norm(tokens_f, norm_gains[0]))
    attention_reduced = low(w_attn)
    query = both_ways(jnp.dot(normed, attention_reduced[0], precision=PRECISE) + attn_biases[0])
    keyset = both_ways(jnp.dot(normed, attention_reduced[1], precision=PRECISE))
    valueset = both_ways(jnp.dot(normed, attention_reduced[2], precision=PRECISE) + attn_biases[1])
    heads_out = lax.map(jax.checkpoint(attention_forward), (query, keyset, valueset, segment))
    hidden = tokens_f + low_back(jnp.dot(heads_out, low(w_proj), precision=PRECISE)) + attn_biases[2]
    routed = low(rms_norm(hidden, norm_gains[1]))
    logits = jnp.dot(routed, low(w_router), precision=PRECISE)
    chosen = (route_ids[..., None] == jnp.arange(EXPERTS, dtype=jnp.int32)).astype(jnp.float32)
    gate_value = lax.optimization_barrier(jnp.sum(jax.nn.softmax(logits, axis=-1) * chosen, axis=-1, keepdims=True))
    target = route_ids * CAP + slot_ids
    group_ids = jnp.arange(groups, dtype=jnp.int32)[:, None]
    buffer = jnp.zeros((groups, EXPERTS * CAP, D), jnp.float32).at[group_ids, target].set(routed)
    buffer = low_back(buffer)
    expert_rows = buffer.reshape(groups, EXPERTS, CAP, D).transpose(1, 0, 2, 3).reshape(EXPERTS, groups * CAP, D)
    expert_out = lax.map(jax.checkpoint(expert_block), (expert_rows, w_in, w_out))
    returned = expert_out.reshape(EXPERTS, groups, CAP, D).transpose(1, 0, 2, 3).reshape(groups, EXPERTS * CAP, D)
    picked = returned[group_ids, target]
    branch = gate_value * picked
    return (hidden + branch, branch)

def newton(update):
    frobenius = jnp.sqrt(lax.optimization_barrier(jnp.sum(update * update, axis=(-2, -1), keepdims=True)))
    orthogonal = update / (frobenius + 1e-07)
    for iteration in range(NS_STEPS):
        gram_matrix = jnp.einsum('...ik,...jk->...ij', orthogonal, orthogonal, precision=PRECISE)
        polynomial = COEF_B * gram_matrix + COEF_C * jnp.einsum('...ij,...jk->...ik', gram_matrix, gram_matrix, precision=PRECISE)
        orthogonal = COEF_A * orthogonal + jnp.einsum('...ij,...jk->...ik', polynomial, orthogonal, precision=PRECISE)
    return orthogonal

def muon(weight, moment, gradient, rate):
    moment_new = MOMENT * moment + gradient
    update = gradient + MOMENT * moment_new
    orthogonal = newton(update)
    return (weight - rate * math.sqrt(max(weight.shape[-2], weight.shape[-1])) * orthogonal, moment_new)

def vector_step(param_rows, moment, gradient):
    moment_new = VECTOR_DECAY * moment + (1.0 - VECTOR_DECAY) * gradient
    pieces = moment_new.reshape(moment_new.shape[0], -1, HD)
    magnitude = jnp.sqrt(lax.optimization_barrier(jnp.mean(pieces * pieces, axis=-1, keepdims=True)) + 1e-06)
    return (param_rows - VECTOR_RATE * (pieces / magnitude).reshape(moment_new.shape), moment_new)

def reference(tokens, lengths, routes, cotangent, norm_gains, attn_biases, w_attn, w_proj, w_router, w_in, w_out, gains_moment, biases_moment, attn_moment, proj_moment, router_moment, in_moment, out_moment):
    groups = TOKENS // ROWS
    tokens_f = tokens.astype(jnp.float32).reshape(groups, ROWS, D)
    segment = sequence_ids(lengths, ROWS)
    route_ids = routes.reshape(groups, ROWS)
    slot_ids = slot_index(route_ids, EXPERTS)

    def forward(tok, gains_p, biases_p, attn_p, proj_p, router_p, in_p, out_p):
        return layer(tok, gains_p, biases_p, attn_p, proj_p, router_p, in_p, out_p, segment, route_ids, slot_ids)
    output, pullback, branch = jax.vjp(forward, tokens_f, norm_gains, attn_biases, w_attn, w_proj, w_router, w_in, w_out, has_aux=True)
    grads = pullback(cotangent.astype(jnp.float32).reshape(groups, ROWS, D))
    grad_tokens, grad_gains, grad_biases, attention_gradient, grad_proj, grad_router, grad_in, grad_out = grads
    updated_norm_gains, new_gains_moment = vector_step(norm_gains, gains_moment, grad_gains)
    new_biases, new_biases_moment = vector_step(attn_biases, biases_moment, grad_biases)
    new_attn, new_attn_moment = muon(w_attn, attn_moment, attention_gradient, RATE_ATTN)
    new_proj, new_proj_moment = muon(w_proj, proj_moment, grad_proj, RATE_PROJ)
    router_t, router_moment_t = muon(w_router.T, router_moment.T, grad_router.T, RATE_ROUTER)
    new_in, new_in_moment = muon(w_in, in_moment, grad_in, RATE_IN)
    new_out, new_out_moment = muon(w_out, out_moment, grad_out, RATE_OUT)
    layer_out = output.reshape(TOKENS, D).astype(jnp.bfloat16)
    input_grad = grad_tokens.reshape(TOKENS, D)
    expert_branch = branch.reshape(TOKENS, D)
    return (layer_out, input_grad, expert_branch, updated_norm_gains, new_gains_moment, new_biases, new_biases_moment, new_attn, new_attn_moment, new_proj, new_proj_moment, router_t.T, router_moment_t.T, new_in, new_in_moment, new_out, new_out_moment)
```

```python
import math

import jax
import jax.numpy as jnp
from jax import lax
from jax.sharding import PartitionSpec as P

HD = 64
FF = 3072
NS_STEPS = 5


PRECISE = lax.Precision.HIGHEST
MOMENT = 0.95
VECTOR_DECAY = 0.9
VECTOR_RATE = 0.2
COEF_A = 3.4445
COEF_B = -4.775
COEF_C = 2.0315
RATE_ATTN = 0.05
RATE_PROJ = 0.1
RATE_ROUTER = 0.03
RATE_IN = 0.04
RATE_OUT = 0.4


def rms_norm(values, gain_row):
    factor = lax.rsqrt(jnp.mean(values * values, axis=-1, keepdims=True) + 1e-06)
    return values * factor * gain_row


def newton_whole(update):
    frobenius = jnp.sqrt(jnp.sum(update * update, axis=(-2, -1), keepdims=True))
    orthogonal = update / (frobenius + 1e-07)
    for iteration in range(NS_STEPS):
        gram_matrix = jnp.einsum("kif,kjf->kij", orthogonal, orthogonal, precision=PRECISE)
        polynomial = COEF_B * gram_matrix + COEF_C * jnp.einsum(
            "kij,kjl->kil", gram_matrix, gram_matrix, precision=PRECISE
        )
        orthogonal = COEF_A * orthogonal + jnp.einsum(
            "kij,kjf->kif", polynomial, orthogonal, precision=PRECISE
        )
    return orthogonal


def product(spec, left, right):
    return jnp.einsum(
        spec,
        left.astype(jnp.bfloat16),
        right.astype(jnp.bfloat16),
        preferred_element_type=jnp.float32,
    )


def mean_diagonal(matrices, identity):
    return jnp.sum(matrices * identity, axis=(-2, -1), keepdims=True) / identity.shape[-1]


def newton_low(update):
    frobenius = jnp.sqrt(jnp.sum(update * update, axis=(-2, -1), keepdims=True))
    orthogonal = update / (frobenius + 1e-07)
    identity = jnp.eye(update.shape[-2], dtype=jnp.float32)
    for iteration in range(NS_STEPS):
        gram_matrix = product("kif,kjf->kij", orthogonal, orthogonal)
        level = mean_diagonal(gram_matrix, identity)
        rest = gram_matrix - level * identity
        polynomial_rest = (COEF_B + 2.0 * COEF_C * level) * rest + COEF_C * product(
            "kij,kjl->kil", rest, rest
        )
        shift = mean_diagonal(polynomial_rest, identity)
        factor = COEF_A + COEF_B * level + COEF_C * level * level + shift
        orthogonal = factor * orthogonal + product(
            "kij,kjf->kif", polynomial_rest - shift * identity, orthogonal
        )
    return orthogonal


def vector_step(param_rows, moment, gradient):
    moment_new = VECTOR_DECAY * moment + (1.0 - VECTOR_DECAY) * gradient
    pieces = moment_new.reshape(moment_new.shape[0], -1, HD)
    magnitude = jnp.sqrt(jnp.mean(pieces * pieces, axis=-1, keepdims=True) + 1e-06)
    return (param_rows - VECTOR_RATE * (pieces / magnitude).reshape(moment_new.shape), moment_new)


def body(
    tokens,
    lengths,
    routes,
    cotangent,
    norm_gains,
    attn_biases,
    w_attn,
    w_proj,
    w_router,
    w_in,
    w_out,
    gains_moment,
    biases_moment,
    attn_moment,
    proj_moment,
    router_moment,
    in_moment,
    out_moment,
):
    row_count, model_width = tokens.shape
    tensor_count = lax.axis_size("tensor")
    expert_count = lax.axis_size("expert")
    data_count = lax.axis_size("dp")
    tensor_index = lax.axis_index("tensor")
    head_width = w_attn.shape[2]
    local_heads = head_width // HD
    expert_local = w_in.shape[0]
    expert_total = expert_local * expert_count
    capacity = 2 * row_count // expert_total
    block_rows = min(512, row_count)
    block_count = row_count // block_rows
    head_scale = HD ** (-0.5)
    in_low, out_low = (
        lax.all_gather(w_in.astype(jnp.bfloat16), "dp", axis=1, tiled=True),
        lax.all_gather(w_out.astype(jnp.bfloat16), "dp", axis=1, tiled=True),
    )
    seq_ends = jnp.cumsum(lengths[0])
    position = jnp.arange(row_count, dtype=jnp.int32)
    segment = jnp.sum((position[:, None] >= seq_ends[None, :]).astype(jnp.int32), axis=1)
    route_ids = routes[:, 0]
    chosen_int = (route_ids[:, None] == jnp.arange(expert_total, dtype=jnp.int32)[None, :]).astype(
        jnp.int32
    )
    slot_ids = jnp.sum((jnp.cumsum(chosen_int, axis=0) - 1) * chosen_int, axis=1)
    target = (
        route_ids % expert_local * expert_count + route_ids // expert_local
    ) * capacity + slot_ids

    def spread(values):
        return lax.all_gather(values, "tensor", axis=3, tiled=True)

    def dispatch(values_low):
        flat_rows = (
            jnp.zeros((expert_total * capacity, model_width), jnp.bfloat16)
            .at[target]
            .set(values_low)
        )
        grid_rows = flat_rows.reshape(expert_local, expert_count, capacity, model_width)
        arrived = lax.all_to_all(grid_rows, "expert", split_axis=1, concat_axis=1, tiled=True)
        return arrived.reshape(expert_local, expert_count * capacity, model_width)

    def give_back(values):
        grid_rows = values.reshape(expert_local, expert_count, capacity, model_width)
        summed = lax.psum_scatter(
            grid_rows.astype(jnp.bfloat16), "tensor", scatter_dimension=3, tiled=True
        )
        arrived = lax.all_to_all(summed, "expert", split_axis=1, concat_axis=1, tiled=True)
        return spread(arrived).reshape(expert_total * capacity, model_width)[target]

    x_float = tokens.astype(jnp.float32)
    normed, norm_back = jax.vjp(rms_norm, x_float, norm_gains[0])
    normalized_reduced = normed.astype(jnp.bfloat16)
    attention_reduced = w_attn.astype(jnp.bfloat16)
    own_bias = lax.dynamic_slice_in_dim(attn_biases[:2], tensor_index * head_width, head_width, 1)
    projected_output = jnp.einsum(
        "kj,bjc->bkc", normalized_reduced, attention_reduced, preferred_element_type=jnp.float32
    )
    query_low = (projected_output[0] + own_bias[0]).astype(jnp.bfloat16)
    key_low = projected_output[1].astype(jnp.bfloat16)
    value_low = (projected_output[2] + own_bias[1]).astype(jnp.bfloat16)
    key_heads = key_low.reshape(row_count, local_heads, HD)
    value_heads = value_low.reshape(row_count, local_heads, HD)
    query_blocks = query_low.reshape(block_count, block_rows, local_heads, HD)
    segment_blocks = segment.reshape(block_count, block_rows)

    def block_scores(query_block, segment_block):
        raw_scores = (
            jnp.einsum("qhd,khd->hqk", query_block, key_heads, preferred_element_type=jnp.float32)
            * head_scale
        )
        same_seq = segment_block[:, None] == segment[None, :]
        return jnp.where(same_seq[None], raw_scores, -1e30)

    def forward_block(pieces):
        query_block, segment_block = pieces
        scores = block_scores(query_block, segment_block)
        weights = jax.nn.softmax(scores, axis=-1)
        log_total = jax.nn.logsumexp(scores, axis=-1)
        heads_part = jnp.einsum(
            "hqk,khd->qhd",
            weights.astype(jnp.bfloat16),
            value_heads,
            preferred_element_type=jnp.float32,
        )
        return (heads_part.astype(jnp.bfloat16), log_total)

    head_blocks, log_totals = lax.map(forward_block, (query_blocks, segment_blocks))
    heads_low = head_blocks.reshape(row_count, head_width)
    proj_low = w_proj.astype(jnp.bfloat16)
    attn_part = jnp.dot(heads_low, proj_low, preferred_element_type=jnp.float32)
    attn_full = lax.psum(attn_part, "tensor")
    hidden = x_float + attn_full + attn_biases[2]
    routed, routed_back = jax.vjp(rms_norm, hidden, norm_gains[1])
    routed_low = routed.astype(jnp.bfloat16)
    router_low = w_router.astype(jnp.bfloat16)
    logits = jnp.dot(routed_low, router_low, preferred_element_type=jnp.float32)
    chosen = chosen_int.astype(jnp.float32)

    def gate_of(logit_rows):
        return jnp.sum(jax.nn.softmax(logit_rows, axis=-1) * chosen, axis=-1, keepdims=True)

    gate_value, gate_back = jax.vjp(gate_of, logits)
    expert_rows = dispatch(routed_low)
    preact = jnp.einsum("jrd,jdf->jrf", expert_rows, in_low, preferred_element_type=jnp.float32)
    activation, gelu_back = jax.vjp(jax.nn.gelu, preact)
    act_low = activation.astype(jnp.bfloat16)
    expert_part = jnp.einsum("jrf,jdf->jrd", act_low, out_low, preferred_element_type=jnp.float32)
    picked = give_back(expert_part).astype(jnp.float32)
    expert_branch = gate_value * picked
    layer_out = (hidden + expert_branch).astype(jnp.bfloat16)
    grad_rows = cotangent.astype(jnp.float32)
    back_gate = jnp.sum(grad_rows * picked, axis=1, keepdims=True)
    back_logits = gate_back(back_gate)[0]
    back_picked = (gate_value * grad_rows).astype(jnp.bfloat16)
    back_expert = dispatch(back_picked)
    back_act = jnp.einsum("jrd,jdf->jrf", back_expert, out_low, preferred_element_type=jnp.float32)
    back_preact = gelu_back(back_act)[0].astype(jnp.bfloat16)
    grad_out_w = jnp.einsum(
        "jrd,jrf->jdf", back_expert, act_low, preferred_element_type=jnp.float32
    )
    grad_in_w = jnp.einsum(
        "jrd,jrf->jdf", expert_rows, back_preact, preferred_element_type=jnp.float32
    )
    back_rows = jnp.einsum("jrf,jdf->jrd", back_preact, in_low, preferred_element_type=jnp.float32)
    back_routed = give_back(back_rows).astype(jnp.float32) + jnp.dot(
        back_logits, router_low.astype(jnp.float32).T, precision=PRECISE
    )
    grad_router = jnp.dot(routed_low.astype(jnp.float32).T, back_logits, precision=PRECISE)
    hidden_norm_grad, grad_gain_two = routed_back(back_routed)
    hidden_grad = grad_rows + hidden_norm_grad
    grad_bias_out = jnp.sum(hidden_grad, axis=0)
    hidden_grad_low = hidden_grad.astype(jnp.bfloat16)
    grad_proj = jnp.einsum(
        "rf,rd->fd", heads_low, hidden_grad_low, preferred_element_type=jnp.float32
    )
    heads_grad_low = jnp.einsum(
        "rd,fd->rf", hidden_grad_low, proj_low, preferred_element_type=jnp.float32
    ).astype(jnp.bfloat16)
    heads_grad_blocks = heads_grad_low.reshape(block_count, block_rows, local_heads, HD)

    def backward_block(carry, pieces):
        key_acc, value_acc = carry
        query_block, segment_block, grad_block, log_total = pieces
        scores = block_scores(query_block, segment_block)
        weights = jnp.exp(scores - log_total[:, :, None])
        value_acc = value_acc + jnp.einsum(
            "hqk,qhd->khd",
            weights.astype(jnp.bfloat16),
            grad_block,
            preferred_element_type=jnp.float32,
        )
        grad_weights = jnp.einsum(
            "qhd,khd->hqk", grad_block, value_heads, preferred_element_type=jnp.float32
        )
        grad_scores = (
            weights * (grad_weights - jnp.sum(grad_weights * weights, axis=-1, keepdims=True))
        ).astype(jnp.bfloat16)
        grad_query = (
            jnp.einsum("hqk,khd->qhd", grad_scores, key_heads, preferred_element_type=jnp.float32)
            * head_scale
        )
        key_acc = (
            key_acc
            + jnp.einsum(
                "hqk,qhd->khd", grad_scores, query_block, preferred_element_type=jnp.float32
            )
            * head_scale
        )
        return ((key_acc, value_acc), grad_query.astype(jnp.bfloat16))

    zero_heads = jnp.zeros((row_count, local_heads, HD), jnp.float32)
    (key_total, value_total), query_grads = lax.scan(
        backward_block,
        (zero_heads, zero_heads),
        (query_blocks, segment_blocks, heads_grad_blocks, log_totals),
    )
    query_grad = query_grads.reshape(row_count, head_width)
    key_grad = key_total.reshape(row_count, head_width).astype(jnp.bfloat16)
    value_grad = value_total.reshape(row_count, head_width).astype(jnp.bfloat16)
    query_key_value_gradient = jnp.stack([query_grad, key_grad, value_grad])
    attention_gradient = jnp.einsum(
        "gy,egz->eyz",
        normalized_reduced,
        query_key_value_gradient,
        preferred_element_type=jnp.float32,
    )
    normalized_gradient = jnp.einsum(
        "txp,tgp->xg",
        query_key_value_gradient,
        attention_reduced,
        preferred_element_type=jnp.float32,
    )
    own_bias_grad = jnp.stack(
        [
            jnp.sum(query_grad, axis=0, dtype=jnp.float32),
            jnp.sum(value_grad, axis=0, dtype=jnp.float32),
        ]
    )
    bias_padded = lax.dynamic_update_slice_in_dim(
        jnp.zeros((2, model_width), jnp.float32), own_bias_grad, tensor_index * head_width, 1
    )
    normalized_gradient, bias_pair = (
        lax.psum(normalized_gradient.astype(jnp.bfloat16), "tensor").astype(jnp.float32),
        lax.psum(bias_padded.astype(jnp.bfloat16), "tensor").astype(jnp.float32),
    )
    input_norm_grad, grad_gain_one = norm_back(normalized_gradient)
    input_grad = hidden_grad + input_norm_grad
    gain_grads = jnp.stack([grad_gain_one, grad_gain_two])
    bias_grads = jnp.stack([bias_pair[0], bias_pair[1], grad_bias_out])
    dense_gradient = jnp.concatenate([attention_gradient, grad_proj.T[None]], axis=0)
    dense_gradient = lax.psum(dense_gradient.astype(jnp.bfloat16), ("expert", "dp")).astype(
        jnp.float32
    )
    attention_gradient, grad_proj = (dense_gradient[:3], dense_gradient[3].T)
    small_grads = lax.psum(
        jnp.concatenate([gain_grads, bias_grads, grad_router.T], axis=0), ("expert", "dp")
    )
    gain_grads, bias_grads, grad_router = (small_grads[:2], small_grads[2:5], small_grads[5:].T)
    grad_in_w, grad_out_w = (
        lax.psum_scatter(
            grad_in_w.astype(jnp.bfloat16), "dp", scatter_dimension=1, tiled=True
        ).astype(jnp.float32),
        lax.psum_scatter(
            grad_out_w.astype(jnp.bfloat16), "dp", scatter_dimension=1, tiled=True
        ).astype(jnp.float32),
    )
    updated_norm_gains, new_gains_moment = vector_step(norm_gains, gains_moment, gain_grads)
    new_biases, new_biases_moment = vector_step(attn_biases, biases_moment, bias_grads)
    attn_moment_new = MOMENT * attn_moment + attention_gradient
    attn_update = attention_gradient + MOMENT * attn_moment_new
    proj_moment_new = MOMENT * proj_moment + grad_proj
    proj_update = grad_proj + MOMENT * proj_moment_new
    dense_stack = jnp.concatenate([attn_update, proj_update.T[None]], axis=0)
    owned = lax.all_to_all(
        dense_stack.astype(jnp.bfloat16), "tensor", split_axis=0, concat_axis=2, tiled=True
    ).astype(jnp.float32)
    settled = lax.all_to_all(
        newton_low(owned).astype(jnp.bfloat16), "tensor", split_axis=2, concat_axis=0, tiled=True
    ).astype(jnp.float32)
    dense_factor = math.sqrt(model_width)
    new_attn = w_attn - RATE_ATTN * dense_factor * settled[:3]
    new_proj = w_proj - RATE_PROJ * dense_factor * settled[3].T
    router_moment_new = MOMENT * router_moment + grad_router
    router_update = grad_router + MOMENT * router_moment_new
    router_ortho = newton_whole(router_update.T[None])[0].T
    new_router = w_router - RATE_ROUTER * math.sqrt(max(model_width, expert_total)) * router_ortho
    in_moment_new = MOMENT * in_moment + grad_in_w
    in_update = grad_in_w + MOMENT * in_moment_new
    out_moment_new = MOMENT * out_moment + grad_out_w
    out_update = grad_out_w + MOMENT * out_moment_new
    expert_stack = jnp.concatenate([in_update, out_update], axis=0)
    stack_count, row_part, col_part = expert_stack.shape
    slot_total = data_count * tensor_count
    filler = jnp.zeros((slot_total - stack_count, row_part, col_part), jnp.float32)
    padded = jnp.concatenate([expert_stack, filler], axis=0).reshape(
        data_count, tensor_count, row_part, col_part
    )
    whole_matrix = lax.all_to_all(
        lax.all_to_all(padded.astype(jnp.bfloat16), "dp", split_axis=0, concat_axis=2, tiled=True),
        "tensor",
        split_axis=1,
        concat_axis=3,
        tiled=True,
    ).astype(padded.dtype)
    whole_ortho = newton_low(whole_matrix.reshape(1, model_width, tensor_count * col_part))
    ortho_low = whole_ortho.astype(jnp.bfloat16).reshape(
        data_count, row_part, tensor_count * col_part
    )
    column_parts = jnp.stack(
        [ortho_low[:, :, t * col_part : (t + 1) * col_part] for t in range(tensor_count)]
    )
    own_columns = lax.all_to_all(
        column_parts, "tensor", split_axis=0, concat_axis=0, tiled=True
    )
    returned = lax.all_to_all(own_columns, "dp", split_axis=1, concat_axis=1, tiled=True)
    expert_ortho = jnp.stack(
        [returned[m % tensor_count, m // tensor_count] for m in range(stack_count)]
    ).astype(jnp.float32)
    expert_factor = math.sqrt(max(model_width, FF))
    new_in = w_in - RATE_IN * expert_factor * expert_ortho[:expert_local]
    new_out = w_out - RATE_OUT * expert_factor * expert_ortho[expert_local:]
    return (
        layer_out,
        input_grad,
        expert_branch,
        updated_norm_gains,
        new_gains_moment,
        new_biases,
        new_biases_moment,
        new_attn,
        attn_moment_new,
        new_proj,
        proj_moment_new,
        new_router,
        router_moment_new,
        new_in,
        in_moment_new,
        new_out,
        out_moment_new,
    )


def solution(mesh):
    return jax.shard_map(
        body,
        mesh=mesh,
        in_specs=(
            P(("expert", "dp"), None),
            P(("expert", "dp"), None),
            P(("expert", "dp"), None),
            P(("expert", "dp"), None),
            P(),
            P(),
            P(None, None, "tensor"),
            P("tensor", None),
            P(),
            P("expert", "dp", "tensor"),
            P("expert", "dp", "tensor"),
            P(),
            P(),
            P(None, None, "tensor"),
            P("tensor", None),
            P(),
            P("expert", "dp", "tensor"),
            P("expert", "dp", "tensor"),
        ),
        out_specs=(
            P(("expert", "dp"), None),
            P(("expert", "dp"), None),
            P(("expert", "dp"), None),
            P(),
            P(),
            P(),
            P(),
            P(None, None, "tensor"),
            P(None, None, "tensor"),
            P("tensor", None),
            P("tensor", None),
            P(),
            P(),
            P("expert", "dp", "tensor"),
            P("expert", "dp", "tensor"),
            P("expert", "dp", "tensor"),
            P("expert", "dp", "tensor"),
        ),
        check_vma=False,
    )
```
